256 devices in a mesh: shard: 64 (over y_lo, z, x), node: 4 (over y_hi, core).
Axes of the slice: x: 4, y: 4 (y_hi: 2, y_lo: 2; y = y_hi * 2 + y_lo), z: 8, core: 2. Of those that a mesh axis runs over, the one named last changes fastest.
Arguments:
- inputs: bfloat16 [2, 32768, 8192], P(None, ('shard', 'node')), may hold values from -24 to 24
- key_weight: bfloat16 [8192, 512], P(('node', 'shard')), may hold values from -0.0625 to 0.0625
- key_cotangent: bfloat16 [2, 32768, 512], P(None, ('shard', 'node')), may hold values from -12 to 12
Outputs:
- key_out: bfloat16 [2, 32768, 512], P(None, ('shard', 'node'))
- input_grad: bfloat16 [2, 32768, 8192], P(None, ('shard', 'node'))
- weight_grad: float32 [8192, 512], P(('node', 'shard'))
The draws below stay inside these ranges and needn't reach their ends.
All inputs are finite; a program needn't handle non-finite values.
Results may differ from the reference program's by a relative error of at most 0.001.
Values may be sent and summed in bfloat16 or wider, within the bound.
A program may use at most 128 MiB of HBM per device.

```python
import jax
import jax.numpy as jnp
from jax import lax

D = 8192
HEAD = 128
KV_HEADS = 4
MICRO = 2
KEY_WIDTH = 512
TOKENS = 32768


def raised(drawn, key, source, target, blocks, factor):
    def block_of(dim):
        return (jnp.arange(drawn.shape[dim]) // (drawn.shape[dim] // blocks)).reshape((-1,) + (1,) * (drawn.ndim - 1 - dim))

    near = jax.random.permutation(key, blocks)[block_of(target)]
    second = (block_of(target) + blocks // 2) % blocks
    return jnp.where((block_of(source) == near) | (block_of(source) == second), factor * drawn, drawn)


def steps_of(own_key, shape, cuts, smallest, largest):
    loudness = 1.0
    for axis_at, parts in cuts:
        steps = jax.random.uniform(jax.random.fold_in(jax.random.fold_in(own_key, 6), axis_at), (parts,), jnp.float32, smallest / len(cuts), largest / len(cuts))
        loudness = loudness * jnp.repeat(jnp.exp(steps), shape[axis_at] // parts).reshape((-1,) + (1,) * (len(shape) - 1 - axis_at))
    return loudness


def gaussian(stream_key, extent, width, limit, split=(), kind=jnp.bfloat16):
    level = steps_of(stream_key, extent, split, -0.22, 0.18) if split else 1.0
    drawn = jax.random.normal(stream_key, extent, jnp.float32) * width * level
    return jnp.minimum(jnp.maximum(drawn, -limit), limit).astype(kind)


def bell_draw_with(key, extent, spread, limit, pieces, heavy, dtype=jnp.bfloat16):
    values = spread * jax.random.normal(key, extent, jnp.float32)
    if pieces:
        values = values * steps_of(key, extent, pieces, -0.22, 0.18)
    return jnp.clip(raised(values, jax.random.fold_in(key, 3), *heavy), -limit, limit).astype(dtype)


def setup_inputs(seed: int = 0) -> dict:
    splits = jax.random.split(jax.random.key(seed), 4)
    return {
        "inputs": bell_draw_with(splits[0], (MICRO, TOKENS, D), 1.0, 24.0, ((1, 256),), (1, 2, 256, 6.0)),
        "key_weight": gaussian(splits[1], (D, KEY_WIDTH), D ** -0.5, 0.0625, ((0, 256),)),
        "key_cotangent": gaussian(splits[2], (MICRO, TOKENS, KEY_WIDTH), 2.0, 12.0, ((1, 256),)),
    }


def reference(inputs, key_weight, key_cotangent):
    key_list = []
    grad_list = []
    weight_grad = jnp.zeros((D, KV_HEADS * HEAD), jnp.float32)
    for micro_index in range(MICRO):
        token_rows = inputs[micro_index]
        cotangent = key_cotangent[micro_index]
        key_list.append(jnp.dot(token_rows, key_weight, preferred_element_type=jnp.float32).astype(jnp.bfloat16))
        grad_list.append(lax.dot_general(cotangent, key_weight, (((1,), (1,)), ((), ())), preferred_element_type=jnp.float32).astype(jnp.bfloat16))
        weight_grad = weight_grad + lax.dot_general(token_rows, cotangent, (((0,), (0,)), ((), ())), preferred_element_type=jnp.float32)
    factor = float(MICRO * TOKENS) ** -0.5
    return jnp.stack(key_list), jnp.stack(grad_list), weight_grad * factor
```

```python
import jax
import jax.numpy as jnp
from jax import lax
from jax.experimental import pallas as pl
from jax.experimental.pallas import tpu as pltpu
from jax.sharding import PartitionSpec as P

MESH = pl.DeviceIdType.MESH
F32 = jnp.float32
BF16 = jnp.bfloat16
ALL = slice(None)

NX, NY, NZ = 4, 4, 8
ROWS = 32


def place():
    s = lax.axis_index("shard")
    n = lax.axis_index("node")
    x = lax.rem(s, NX)
    z = lax.rem(s // NX, NZ)
    y = (n // 2) * 2 + s // (NX * NZ)
    return x, y, z, lax.rem(n, 2)


def device(x, y, z, c):
    return (lax.rem(y, 2) * (NX * NZ) + z * NX + x, (y // 2) * 2 + c)


PART_A = (pl.ds(0, 16), pl.ds(0, 384))
PART_B = (pl.ds(16, 16), pl.ds(0, 384))
PART_AB = (pl.ds(0, 32), pl.ds(0, 384))
PART_C = (pl.ds(0, 32), pl.ds(384, 128))

SEMS = 128


def kernel(inputs, weight, cot, key_out, input_grad, weight_grad,
           xs, cs, ws, grad, acc, key_in, stage,
           ra1, rb1, rc1, ra2, rb2, rc2, rab3, rc3,
           send, recv, local):
    x, y, z, c = place()
    factor = 1.0 / 256.0
    counter = [0]
    started = []

    def px(k):
        return lax.rem(x + k + 4 * NX, NX)

    def py(k):
        return lax.rem(y + k + 4 * NY, NY)

    def pz(k):
        return lax.rem(z + k + 4 * NZ, NZ)

    def to(axis, k):
        if axis == "x":
            return device(px(k), y, z, c)
        if axis == "y":
            return device(x, py(k), z, c)
        if axis == "z":
            return device(x, y, pz(k), c)
        return device(x, y, z, 1 - c)

    def remote(src, dst, target):
        i = counter[0]
        counter[0] += 1
        copy = pltpu.make_async_remote_copy(
            src_ref=src, dst_ref=dst, send_sem=send.at[i], recv_sem=recv.at[i],
            device_id=target, device_id_type=MESH)
        copy.start()
        started.append(copy)
        return copy

    barrier = pltpu.get_barrier_semaphore()
    partners = [("x", k) for k in range(1, NX)] + [("y", k) for k in range(1, NY)]
    partners += [("z", k) for k in range(1, NZ)] + [("c", 1)]
    for axis, k in partners:
        pl.semaphore_signal(barrier, inc=1, device_id=to(axis, k), device_id_type=MESH)

    def strip(half, core):
        return pl.ds(pl.multiple_of(half * 4096 + core * 2048, 2048), 2048)

    own = []
    for half in range(2):
        own.append(pltpu.make_async_copy(
            inputs.at[:, :, strip(half, c)], xs.at[0, :, :, pl.ds(half * 2048, 2048)], local.at[half]))
    own.append(pltpu.make_async_copy(cot, cs.at[0], local.at[2]))
    for copy in own:
        copy.start()
    wcopy = pltpu.make_async_copy(weight, ws.at[y, z, x], local.at[3])
    wcopy.start()

    pl.semaphore_wait(barrier, len(partners))

    g1ab = [remote(weight.at[PART_AB], ws.at[(y, z, x) + PART_AB], to("z", k)) for k in range(1, NZ)]
    g1c = [remote(weight.at[PART_C], ws.at[(y, z, x) + PART_C], to("x", k)) for k in range(1, NX)]
    pair = [remote(cot, cs.at[1], to("c", 1))]
    for half in range(2):
        pair.append(remote(inputs.at[:, :, strip(half, 1 - c)],
                           xs.at[1, :, :, pl.ds(half * 2048, 2048)], to("c", 1)))

    def received(copies):
        for copy in copies:
            copy.wait_recv()

    wcopy.wait()
    received(g1c)
    ref = ws.at[(y, z, ALL) + PART_C]
    g2c = [remote(ref, ref, to("y", k)) for k in range(1, NY)]
    received(g1ab)
    ref = ws.at[(y, ALL, x) + PART_A]
    g2a = [remote(ref, ref, to("y", k)) for k in range(1, NY)]
    ref = ws.at[(y, ALL, x) + PART_B]
    g2b = [remote(ref, ref, to("x", k)) for k in range(1, NX)]

    for copy in own:
        copy.wait()
    received(pair)

    def gradient(yy):
        @pl.loop(0, 2)
        def _(h):
            start = pl.multiple_of(yy * 1024 + h * 512, 512)
            left = xs[:, :, :, pl.ds(start, 512)].reshape(512, 512)
            right = cs[...].reshape(512, 512)
            out = lax.dot_general(left, right, (((0,), (0,)), ((), ())), preferred_element_type=F32)
            grad[yy, pl.ds(h * 4, 4)] = out.reshape(4, NX, ROWS, 512)

    d = 1 - 2 * c

    def ga(k):
        return grad.at[(ALL, ALL, px(k)) + PART_A]

    def gb(k):
        return grad.at[(py(k), ALL, ALL) + PART_B]

    def gc(k):
        return grad.at[(ALL, pz(k), ALL) + PART_C]

    gradient(py(2))
    b_far = remote(gb(2), rb1.at[0], to("y", d))
    gradient(py(-d))
    b_near = remote(gb(-d), rb1.at[1], to("y", -d))
    gradient(py(d))
    gradient(y)
    a_far = remote(ga(2), ra1.at[0], to("x", d))
    c_up = [remote(gc(4), rc1.at[0], to("z", d))]
    c_down = [remote(gc(-3 * d), rc1.at[4], to("z", -d))]
    a_near = remote(ga(-d), ra1.at[1], to("x", -d))

    received(g2c)
    def wc(k):
        return ws.at[(ALL, pz(k), ALL) + PART_C]
    def wa(k):
        return ws.at[(ALL, ALL, px(k)) + PART_A]
    def wb(k):
        return ws.at[(py(k), ALL, ALL) + PART_B]
    g3c_up = [remote(wc(0), wc(0), to("z", d))]
    g3c_down = [remote(wc(0), wc(0), to("z", -d))]
    received(g2a)
    g3a_up = [remote(wa(0), wa(0), to("x", d))]
    g3a_down = [remote(wa(0), wa(0), to("x", -d))]
    received(g2b)
    g3b_up = [remote(wb(0), wb(0), to("y", d))]
    g3b_down = [remote(wb(0), wb(0), to("y", -d))]

    def add_a(k, terms):
        xx = px(k)

        @pl.loop(0, NY)
        def _(i):
            total = grad[(i, ALL, xx) + PART_A]
            for t in terms:
                total = total + ra1[t, i]
            grad[(i, ALL, xx) + PART_A] = total

    def add_b(k, terms):
        yy = py(k)

        @pl.loop(0, NX)
        def _(i):
            total = grad[(yy, ALL, i) + PART_B]
            for t in terms:
                total = total + rb1[t, :, i]
            grad[(yy, ALL, i) + PART_B] = total

    def add_c(k, terms):
        zz = pz(k)

        @pl.loop(0, NY)
        def _(i):
            total = grad[(i, zz, ALL) + PART_C]
            for t in terms:
                total = total + rc1[t, i]
            grad[(i, zz, ALL) + PART_C] = total

    def step_c(i):
        c_up[-1].wait_recv()
        add_c((4 - i) * d, [i - 1])
        c_up.append(remote(gc((4 - i) * d), rc1.at[i], to("z", d)))
        if i < 3:
            c_down[-1].wait_recv()
            add_c(-(3 - i) * d, [3 + i])
            c_down.append(remote(gc(-(3 - i) * d), rc1.at[4 + i], to("z", -d)))

    def forward_c(i):
        g3c_up[-1].wait_recv()
        g3c_up.append(remote(wc(-i * d), wc(-i * d), to("z", d)))
        if i < 3:
            g3c_down[-1].wait_recv()
            g3c_down.append(remote(wc(i * d), wc(i * d), to("z", -d)))

    step_c(1)
    b_far.wait_recv()
    add_b(d, [0])
    b_last = remote(gb(d), rb1.at[2], to("y", d))
    step_c(2)
    a_far.wait_recv()
    add_a(d, [0])
    a_last = remote(ga(d), ra1.at[2], to("x", d))
    forward_c(1)
    step_c(3)
    g3a_up[-1].wait_recv()
    g3a_up.append(remote(wa(-d), wa(-d), to("x", d)))
    g3b_up[-1].wait_recv()
    g3b_up.append(remote(wb(-d), wb(-d), to("y", d)))
    forward_c(2)

    b_near.wait_recv()
    b_last.wait_recv()
    add_b(0, [1, 2])
    s2b = [remote(grad.at[(y, ALL, px(k)) + PART_B], rb2.at[k - 1], to("x", k)) for k in range(1, NX)]
    a_near.wait_recv()
    a_last.wait_recv()
    add_a(0, [1, 2])
    s2a = [remote(grad.at[(py(k), ALL, x) + PART_A], ra2.at[k - 1], to("y", k)) for k in range(1, NY)]
    c_up[-1].wait_recv()
    c_down[-1].wait_recv()
    add_c(0, [3, 6])
    s2c = [remote(grad.at[(py(k), z, ALL) + PART_C], rc2.at[k - 1], to("y", k)) for k in range(1, NY)]
    forward_c(3)

    received(s2b)
    grad[(y, ALL, x) + PART_B] = grad[(y, ALL, x) + PART_B] + (rb2[0] + rb2[1] + rb2[2])
    received(s2a)
    grad[(y, ALL, x) + PART_A] = grad[(y, ALL, x) + PART_A] + (ra2[0] + ra2[1] + ra2[2])
    s3ab = [remote(grad.at[(y, pz(k), x) + PART_AB], rab3.at[k - 1], to("z", k)) for k in range(1, NZ)]
    received(s2c)
    grad[(y, z, ALL) + PART_C] = grad[(y, z, ALL) + PART_C] + (rc2[0] + rc2[1] + rc2[2])
    s3c = [remote(grad.at[(y, z, px(k)) + PART_C], rc3.at[k - 1], to("x", k)) for k in range(1, NX)]

    for ring in (g3a_up, g3a_down, g3b_up, g3b_down):
        ring[-1].wait_recv()
    g3c_up[-1].wait_recv()
    g3c_down[-1].wait_recv()

    acc[...] = jnp.zeros_like(acc)

    @pl.loop(0, NY)
    def _(i):
        left = xs[:, :, :, pl.ds(pl.multiple_of(i * 1024, 1024), 1024)].reshape(512, 1024)
        right = ws[i].reshape(1024, 512)
        acc[...] += jnp.dot(left, right, preferred_element_type=F32).reshape(2, 2, 128, 512)

    key_pair = remote(acc.at[1], key_in, to("c", 1))

    outs = []
    for i in range(NY):
        @pl.loop(0, 2)
        def _(h):
            right = ws[i, pl.ds(h * 4, 4)].reshape(512, 512)
            out = lax.dot_general(cs[...].reshape(512, 512), right, (((1,), (1,)), ((), ())),
                                  preferred_element_type=F32).astype(BF16)
            stage[:, :, :, pl.ds(pl.multiple_of(i * 1024 + h * 512, 512), 512)] = out.reshape(2, 2, 128, 512)

        here = pl.ds(i * 1024, 1024)
        there = pl.ds(pl.multiple_of((i // 2) * 4096 + c * 2048 + (i % 2) * 1024, 1024), 1024)
        outs.append(remote(stage.at[1, :, :, here], input_grad.at[:, :, there], to("c", 1)))
        copy = pltpu.make_async_copy(stage.at[0, :, :, here], input_grad.at[:, :, there], local.at[4 + i])
        copy.start()
        own_out = copy
        outs.append(own_out)

    received(s3c)
    received(s3ab)
    rows_ab = grad[(y, z, x) + PART_AB]
    for k in range(NZ - 1):
        rows_ab = rows_ab + rab3[k]
    rows_c = grad[(y, z, x) + PART_C]
    for k in range(NX - 1):
        rows_c = rows_c + rc3[k]
    weight_grad[:, 0:384] = rows_ab * factor
    weight_grad[:, 384:512] = rows_c * factor

    key_pair.wait_recv()
    key_out[...] = (acc[0] + key_in[...]).astype(BF16)

    for i, copy in enumerate(outs):
        if i % 2 == 0:
            copy.wait_recv()
        else:
            copy.wait()
    for copy in started:
        copy.wait_send()


def local(inputs, key_weight, key_cotangent):
    any_spec = pl.BlockSpec(memory_space=pl.ANY)
    vmem_spec = pl.BlockSpec(memory_space=pltpu.VMEM)
    return pl.pallas_call(
        kernel,
        out_shape=(
            jax.ShapeDtypeStruct(key_cotangent.shape, BF16),
            jax.ShapeDtypeStruct(inputs.shape, BF16),
            jax.ShapeDtypeStruct(key_weight.shape, F32),
        ),
        in_specs=[any_spec, vmem_spec, any_spec],
        out_specs=(vmem_spec, any_spec, vmem_spec),
        scratch_shapes=[
            pltpu.VMEM((2, 2, 128, 4096), BF16),
            pltpu.VMEM((2, 2, 128, 512), BF16),
            pltpu.VMEM((NY, NZ, NX, ROWS, 512), BF16),
            pltpu.VMEM((NY, NZ, NX, ROWS, 512), F32),
            pltpu.VMEM((2, 2, 128, 512), F32),
            pltpu.VMEM((2, 128, 512), F32),
            pltpu.VMEM((2, 2, 128, 4096), BF16),
            pltpu.VMEM((3, NY, NZ, 16, 384), F32),
            pltpu.VMEM((3, NZ, NX, 16, 384), F32),
            pltpu.VMEM((7, NY, NX, 32, 128), F32),
            pltpu.VMEM((3, NZ, 16, 384), F32),
            pltpu.VMEM((3, NZ, 16, 384), F32),
            pltpu.VMEM((3, NX, 32, 128), F32),
            pltpu.VMEM((7, 32, 384), F32),
            pltpu.VMEM((3, 32, 128), F32),
            pltpu.SemaphoreType.DMA((SEMS,)),
            pltpu.SemaphoreType.DMA((SEMS,)),
            pltpu.SemaphoreType.DMA((8,)),
        ],
        compiler_params=pltpu.CompilerParams(
            collective_id=0, has_side_effects=True, vmem_limit_bytes=56 * 2**20),
        cost_estimate=pl.CostEstimate(flops=3 * 2 * 256 * 8192 * 512, bytes_accessed=9 * 2**20, transcendentals=0),
        name="key_projection",
    )(inputs, key_weight, key_cotangent)


def solution(mesh):
    tokens = P(None, ("shard", "node"), None)
    rows = P(("node", "shard"), None)
    return jax.shard_map(local, mesh=mesh, in_specs=(tokens, rows, tokens),
                         out_specs=(tokens, tokens, rows), check_vma=False)
```

```python
import jax
import jax.numpy as jnp
from jax import lax
from jax.experimental import pallas as pl
from jax.experimental.pallas import tpu as pltpu
from jax.sharding import PartitionSpec as P

MESH = pl.DeviceIdType.MESH
F32 = jnp.float32
BF16 = jnp.bfloat16
ALL = slice(None)

NX, NY, NZ = 4, 4, 8
ROWS = 32


def place():
    s = lax.axis_index("shard")
    n = lax.axis_index("node")
    x = lax.rem(s, NX)
    z = lax.rem(s // NX, NZ)
    y = (n // 2) * 2 + s // (NX * NZ)
    return x, y, z, lax.rem(n, 2)


def device(x, y, z, c):
    return (lax.rem(y, 2) * (NX * NZ) + z * NX + x, (y // 2) * 2 + c)


PART_A = (pl.ds(0, 16), pl.ds(0, 384))
PART_B = (pl.ds(16, 16), pl.ds(0, 384))
PART_AB = (pl.ds(0, 32), pl.ds(0, 384))
PART_C = (pl.ds(0, 32), pl.ds(384, 128))

SEMS = 128

SCALE = 2.0 ** 8


def encode(value):
    square = value * value
    return ((value * jnp.abs(value)) * (square * SCALE ** 4)).astype(BF16)


def decode(code):
    power = code.astype(F32)
    root = lax.rsqrt(lax.rsqrt(jnp.abs(power))) * (1.0 / SCALE)
    return jnp.where(power < 0, -root, root)


def kernel(inputs, weight, cot, key_out, input_grad, weight_grad,
           xs, cs, ws, grad, acc, key_in, stage,
           ra1, rb1, rc1, ra2, rb2, rc2, rab3, rc3,
           ea1, eb1, ec1, ea2, eb2, ec2,
           send, recv, local):
    x, y, z, c = place()
    factor = 1.0 / 256.0
    counter = [0]
    started = []

    def px(k):
        return lax.rem(x + k + 4 * NX, NX)

    def py(k):
        return lax.rem(y + k + 4 * NY, NY)

    def pz(k):
        return lax.rem(z + k + 4 * NZ, NZ)

    def to(axis, k):
        if axis == "x":
            return device(px(k), y, z, c)
        if axis == "y":
            return device(x, py(k), z, c)
        if axis == "z":
            return device(x, y, pz(k), c)
        return device(x, y, z, 1 - c)

    def remote(src, dst, target):
        i = counter[0]
        counter[0] += 1
        copy = pltpu.make_async_remote_copy(
            src_ref=src, dst_ref=dst, send_sem=send.at[i], recv_sem=recv.at[i],
            device_id=target, device_id_type=MESH)
        copy.start()
        started.append(copy)
        return copy

    barrier = pltpu.get_barrier_semaphore()
    partners = [("x", k) for k in range(1, NX)] + [("y", k) for k in range(1, NY)]
    partners += [("z", k) for k in range(1, NZ)] + [("c", 1)]
    for axis, k in partners:
        pl.semaphore_signal(barrier, inc=1, device_id=to(axis, k), device_id_type=MESH)

    def strip(half, core):
        return pl.ds(pl.multiple_of(half * 4096 + core * 2048, 2048), 2048)

    own = []
    for half in range(2):
        own.append(pltpu.make_async_copy(
            inputs.at[:, :, strip(half, c)], xs.at[0, :, :, pl.ds(half * 2048, 2048)], local.at[half]))
    own.append(pltpu.make_async_copy(cot, cs.at[0], local.at[2]))
    for copy in own:
        copy.start()
    wcopy = pltpu.make_async_copy(weight, ws.at[y, z, x], local.at[3])
    wcopy.start()

    pl.semaphore_wait(barrier, len(partners))

    g1ab = [remote(weight.at[PART_AB], ws.at[(y, z, x) + PART_AB], to("z", k)) for k in range(1, NZ)]
    g1c = [remote(weight.at[PART_C], ws.at[(y, z, x) + PART_C], to("x", k)) for k in range(1, NX)]
    pair = [remote(cot, cs.at[1], to("c", 1))]
    for half in range(2):
        pair.append(remote(inputs.at[:, :, strip(half, 1 - c)],
                           xs.at[1, :, :, pl.ds(half * 2048, 2048)], to("c", 1)))

    def received(copies):
        for copy in copies:
            copy.wait_recv()

    wcopy.wait()
    received(g1c)
    ref = ws.at[(y, z, ALL) + PART_C]
    g2c = [remote(ref, ref, to("y", k)) for k in range(1, NY)]
    received(g1ab)
    ref = ws.at[(y, ALL, x) + PART_A]
    g2a = [remote(ref, ref, to("y", k)) for k in range(1, NY)]
    ref = ws.at[(y, ALL, x) + PART_B]
    g2b = [remote(ref, ref, to("x", k)) for k in range(1, NX)]

    for copy in own:
        copy.wait()
    received(pair)

    def gradient(yy):
        @pl.loop(0, 2)
        def _(h):
            start = pl.multiple_of(yy * 1024 + h * 512, 512)
            left = xs[:, :, :, pl.ds(start, 512)].reshape(512, 512)
            right = cs[...].reshape(512, 512)
            out = lax.dot_general(left, right, (((0,), (0,)), ((), ())), preferred_element_type=F32)
            grad[yy, pl.ds(h * 4, 4)] = out.reshape(4, NX, ROWS, 512)

    d = 1 - 2 * c

    def code_a(k, slot):
        xx = px(k)

        @pl.loop(0, NY)
        def _(i):
            ea1[slot, i] = encode(grad[(i, ALL, xx) + PART_A])

        return ea1.at[slot]

    def code_b(k, slot):
        yy = py(k)

        @pl.loop(0, NX)
        def _(i):
            eb1[slot, :, i] = encode(grad[(yy, ALL, i) + PART_B])

        return eb1.at[slot]

    def code_c(k, slot):
        zz = pz(k)

        @pl.loop(0, NY)
        def _(i):
            ec1[slot, i] = encode(grad[(i, zz, ALL) + PART_C])

        return ec1.at[slot]

    gradient(py(2))
    b_far = remote(code_b(2, 0), rb1.at[0], to("y", d))
    gradient(py(-d))
    b_near = remote(code_b(-d, 1), rb1.at[1], to("y", -d))
    gradient(py(d))
    gradient(y)
    a_far = remote(code_a(2, 0), ra1.at[0], to("x", d))
    c_up = [remote(code_c(4, 0), rc1.at[0], to("z", d))]
    c_down = [remote(code_c(-3 * d, 4), rc1.at[4], to("z", -d))]
    a_near = remote(code_a(-d, 1), ra1.at[1], to("x", -d))

    received(g2c)
    def wc(k):
        return ws.at[(ALL, pz(k), ALL) + PART_C]
    def wa(k):
        return ws.at[(ALL, ALL, px(k)) + PART_A]
    def wb(k):
        return ws.at[(py(k), ALL, ALL) + PART_B]
    g3c_up = [remote(wc(0), wc(0), to("z", d))]
    g3c_down = [remote(wc(0), wc(0), to("z", -d))]
    received(g2a)
    g3a_up = [remote(wa(0), wa(0), to("x", d))]
    g3a_down = [remote(wa(0), wa(0), to("x", -d))]
    received(g2b)
    g3b_up = [remote(wb(0), wb(0), to("y", d))]
    g3b_down = [remote(wb(0), wb(0), to("y", -d))]

    def add_a(k, terms):
        xx = px(k)

        @pl.loop(0, NY)
        def _(i):
            total = grad[(i, ALL, xx) + PART_A]
            for t in terms:
                total = total + decode(ra1[t, i])
            grad[(i, ALL, xx) + PART_A] = total

    def add_b(k, terms):
        yy = py(k)

        @pl.loop(0, NX)
        def _(i):
            total = grad[(yy, ALL, i) + PART_B]
            for t in terms:
                total = total + decode(rb1[t, :, i])
            grad[(yy, ALL, i) + PART_B] = total

    def add_c(k, terms):
        zz = pz(k)

        @pl.loop(0, NY)
        def _(i):
            total = grad[(i, zz, ALL) + PART_C]
            for t in terms:
                total = total + decode(rc1[t, i])
            grad[(i, zz, ALL) + PART_C] = total

    def step_c(i):
        c_up[-1].wait_recv()
        add_c((4 - i) * d, [i - 1])
        c_up.append(remote(code_c((4 - i) * d, i), rc1.at[i], to("z", d)))
        if i < 3:
            c_down[-1].wait_recv()
            add_c(-(3 - i) * d, [3 + i])
            c_down.append(remote(code_c(-(3 - i) * d, 4 + i), rc1.at[4 + i], to("z", -d)))

    def forward_c(i):
        g3c_up[-1].wait_recv()
        g3c_up.append(remote(wc(-i * d), wc(-i * d), to("z", d)))
        if i < 3:
            g3c_down[-1].wait_recv()
            g3c_down.append(remote(wc(i * d), wc(i * d), to("z", -d)))

    step_c(1)
    b_far.wait_recv()
    add_b(d, [0])
    b_last = remote(code_b(d, 2), rb1.at[2], to("y", d))
    step_c(2)
    a_far.wait_recv()
    add_a(d, [0])
    a_last = remote(code_a(d, 2), ra1.at[2], to("x", d))
    forward_c(1)
    step_c(3)
    g3a_up[-1].wait_recv()
    g3a_up.append(remote(wa(-d), wa(-d), to("x", d)))
    g3b_up[-1].wait_recv()
    g3b_up.append(remote(wb(-d), wb(-d), to("y", d)))
    forward_c(2)

    b_near.wait_recv()
    b_last.wait_recv()
    add_b(0, [1, 2])
    s2b = []
    for k in range(1, NX):
        eb2[k - 1] = encode(grad[(y, ALL, px(k)) + PART_B])
        s2b.append(remote(eb2.at[k - 1], rb2.at[k - 1], to("x", k)))
    a_near.wait_recv()
    a_last.wait_recv()
    add_a(0, [1, 2])
    s2a = []
    for k in range(1, NY):
        ea2[k - 1] = encode(grad[(py(k), ALL, x) + PART_A])
        s2a.append(remote(ea2.at[k - 1], ra2.at[k - 1], to("y", k)))
    c_up[-1].wait_recv()
    c_down[-1].wait_recv()
    add_c(0, [3, 6])
    s2c = []
    for k in range(1, NY):
        ec2[k - 1] = encode(grad[(py(k), z, ALL) + PART_C])
        s2c.append(remote(ec2.at[k - 1], rc2.at[k - 1], to("y", k)))
    forward_c(3)

    received(s2b)
    grad[(y, ALL, x) + PART_B] = grad[(y, ALL, x) + PART_B] + (decode(rb2[0]) + decode(rb2[1]) + decode(rb2[2]))
    received(s2a)
    grad[(y, ALL, x) + PART_A] = grad[(y, ALL, x) + PART_A] + (decode(ra2[0]) + decode(ra2[1]) + decode(ra2[2]))
    s3ab = [remote(grad.at[(y, pz(k), x) + PART_AB], rab3.at[k - 1], to("z", k)) for k in range(1, NZ)]
    received(s2c)
    grad[(y, z, ALL) + PART_C] = grad[(y, z, ALL) + PART_C] + (decode(rc2[0]) + decode(rc2[1]) + decode(rc2[2]))
    s3c = [remote(grad.at[(y, z, px(k)) + PART_C], rc3.at[k - 1], to("x", k)) for k in range(1, NX)]

    for ring in (g3a_up, g3a_down, g3b_up, g3b_down):
        ring[-1].wait_recv()
    g3c_up[-1].wait_recv()
    g3c_down[-1].wait_recv()

    acc[...] = jnp.zeros_like(acc)

    @pl.loop(0, NY)
    def _(i):
        left = xs[:, :, :, pl.ds(pl.multiple_of(i * 1024, 1024), 1024)].reshape(512, 1024)
        right = ws[i].reshape(1024, 512)
        acc[...] += jnp.dot(left, right, preferred_element_type=F32).reshape(2, 2, 128, 512)

    key_pair = remote(acc.at[1], key_in, to("c", 1))

    outs = []
    for i in range(NY):
        @pl.loop(0, 2)
        def _(h):
            right = ws[i, pl.ds(h * 4, 4)].reshape(512, 512)
            out = lax.dot_general(cs[...].reshape(512, 512), right, (((1,), (1,)), ((), ())),
                                  preferred_element_type=F32).astype(BF16)
            stage[:, :, :, pl.ds(pl.multiple_of(i * 1024 + h * 512, 512), 512)] = out.reshape(2, 2, 128, 512)

        here = pl.ds(i * 1024, 1024)
        there = pl.ds(pl.multiple_of((i // 2) * 4096 + c * 2048 + (i % 2) * 1024, 1024), 1024)
        outs.append(remote(stage.at[1, :, :, here], input_grad.at[:, :, there], to("c", 1)))
        copy = pltpu.make_async_copy(stage.at[0, :, :, here], input_grad.at[:, :, there], local.at[4 + i])
        copy.start()
        own_out = copy
        outs.append(own_out)

    received(s3c)
    received(s3ab)
    rows_ab = grad[(y, z, x) + PART_AB]
    for k in range(NZ - 1):
        rows_ab = rows_ab + rab3[k]
    rows_c = grad[(y, z, x) + PART_C]
    for k in range(NX - 1):
        rows_c = rows_c + rc3[k]
    weight_grad[:, 0:384] = rows_ab * factor
    weight_grad[:, 384:512] = rows_c * factor

    key_pair.wait_recv()
    key_out[...] = (acc[0] + key_in[...]).astype(BF16)

    for i, copy in enumerate(outs):
        if i % 2 == 0:
            copy.wait_recv()
        else:
            copy.wait()
    for copy in started:
        copy.wait_send()


def local(inputs, key_weight, key_cotangent):
    any_spec = pl.BlockSpec(memory_space=pl.ANY)
    vmem_spec = pl.BlockSpec(memory_space=pltpu.VMEM)
    return pl.pallas_call(
        kernel,
        out_shape=(
            jax.ShapeDtypeStruct(key_cotangent.shape, BF16),
            jax.ShapeDtypeStruct(inputs.shape, BF16),
            jax.ShapeDtypeStruct(key_weight.shape, F32),
        ),
        in_specs=[any_spec, vmem_spec, any_spec],
        out_specs=(vmem_spec, any_spec, vmem_spec),
        scratch_shapes=[
            pltpu.VMEM((2, 2, 128, 4096), BF16),
            pltpu.VMEM((2, 2, 128, 512), BF16),
            pltpu.VMEM((NY, NZ, NX, ROWS, 512), BF16),
            pltpu.VMEM((NY, NZ, NX, ROWS, 512), F32),
            pltpu.VMEM((2, 2, 128, 512), F32),
            pltpu.VMEM((2, 128, 512), F32),
            pltpu.VMEM((2, 2, 128, 4096), BF16),
            pltpu.VMEM((3, NY, NZ, 16, 384), BF16),
            pltpu.VMEM((3, NZ, NX, 16, 384), BF16),
            pltpu.VMEM((7, NY, NX, 32, 128), BF16),
            pltpu.VMEM((3, NZ, 16, 384), BF16),
            pltpu.VMEM((3, NZ, 16, 384), BF16),
            pltpu.VMEM((3, NX, 32, 128), BF16),
            pltpu.VMEM((7, 32, 384), F32),
            pltpu.VMEM((3, 32, 128), F32),
            pltpu.VMEM((3, NY, NZ, 16, 384), BF16),
            pltpu.VMEM((3, NZ, NX, 16, 384), BF16),
            pltpu.VMEM((7, NY, NX, 32, 128), BF16),
            pltpu.VMEM((3, NZ, 16, 384), BF16),
            pltpu.VMEM((3, NZ, 16, 384), BF16),
            pltpu.VMEM((3, NX, 32, 128), BF16),
            pltpu.SemaphoreType.DMA((SEMS,)),
            pltpu.SemaphoreType.DMA((SEMS,)),
            pltpu.SemaphoreType.DMA((8,)),
        ],
        compiler_params=pltpu.CompilerParams(
            collective_id=0, has_side_effects=True, vmem_limit_bytes=47 * 2**20),
        cost_estimate=pl.CostEstimate(flops=3 * 2 * 256 * 8192 * 512, bytes_accessed=9 * 2**20, transcendentals=0),
        name="key_projection",
    )(inputs, key_weight, key_cotangent)


def solution(mesh):
    tokens = P(None, ("shard", "node"), None)
    rows = P(("node", "shard"), None)
    return jax.shard_map(local, mesh=mesh, in_specs=(tokens, rows, tokens),
                         out_specs=(tokens, tokens, rows), check_vma=False)
```

```python
import functools

import jax
import jax.numpy as jnp
from jax import lax
from jax.experimental import pallas as pl
from jax.experimental.pallas import tpu as pltpu
from jax.sharding import PartitionSpec as P

MESH = pl.DeviceIdType.MESH
F32 = jnp.float32
BF16 = jnp.bfloat16
ALL = slice(None)

NX, NY, NZ = 4, 4, 8
ROWS = 32


def place():
    s = lax.axis_index("shard")
    n = lax.axis_index("node")
    x = lax.rem(s, NX)
    z = lax.rem(s // NX, NZ)
    y = (n // 2) * 2 + s // (NX * NZ)
    return x, y, z, lax.rem(n, 2)


def device(x, y, z, c):
    return (lax.rem(y, 2) * (NX * NZ) + z * NX + x, (y // 2) * 2 + c)


PART_A = (pl.ds(0, 16), pl.ds(0, 384))
PART_B = (pl.ds(16, 16), pl.ds(0, 384))
PART_AB = (pl.ds(0, 32), pl.ds(0, 384))
PART_C = (pl.ds(0, 32), pl.ds(384, 128))

SEMS = 176

SCALE = 2.0 ** 8


def encode(value):
    square = value * value
    return ((value * jnp.abs(value)) * (square * SCALE ** 4)).astype(BF16)


def decode(code):
    power = code.astype(F32)
    root = lax.rsqrt(lax.rsqrt(jnp.abs(power))) * (1.0 / SCALE)
    return jnp.where(power < 0, -root, root)


ORDER = (
    "start", "hC", "m0", "hA", "uC01", "gC1", "m1", "m2", "hB", "dC01", "m3", "uC11", "uA01", "rA0",
    "rB0", "gC2", "c21", "c01", "rB3", "rB1", "rB2", "gC3", "c11", "uC02", "rA1", "c31", "gB1",
    "c22", "dC02", "gA1", "c02", "dC11", "uC21", "c12", "uC12", "uC31", "fB0", "rA3", "uC22", "rA2",
    "gA2", "dC12", "c23", "fA0", "c32", "gB3", "c03", "uA11", "fB1", "uC03", "uC32", "c13", "fA1",
    "gB2", "dC21", "uC13", "fB3", "dC31", "fA3", "c33", "fC0", "fA2", "fB2", "uB01", "gA3", "uB11",
    "dC22", "uA21", "k0", "i0", "uC33", "dC32", "uC23", "uB31", "fC3", "k1", "uB21", "fC1", "sB",
    "fC2", "uA31", "sA", "t", "i1", "k2", "i2", "k3", "sC", "i3", "end", "z",
)


def kernel(inputs, weight, cot, key_out, input_grad, weight_grad,
           xs, cs, ws, grad, acc, key_in, stage,
           ra1, rb1, rc1, ra2, rb2, rc2, rab3, rc3,
           ea1, eb1, ec1, ea2, eb2, ec2, eab3, ec3,
           send, recv, local):
    x, y, z, c = place()
    d = 1 - 2 * c
    factor = 1.0 / 256.0

    def px(k):
        return lax.rem(x + k + 4 * NX, NX)

    def py(k):
        return lax.rem(y + k + 4 * NY, NY)

    def pz(k):
        return lax.rem(z + k + 4 * NZ, NZ)

    def to(axis, k):
        if axis == "x":
            return device(px(k), y, z, c)
        if axis == "y":
            return device(x, py(k), z, c)
        if axis == "z":
            return device(x, y, pz(k), c)
        return device(x, y, z, 1 - c)

    axes = {"A": ("x", "y", "z"), "B": ("y", "x", "z"), "C": ("z", "y", "x")}
    at_axis = {"x": px, "y": py, "z": pz}

    def at(part, first, second, third=ALL):
        first = at_axis[axes[part][0]](first)
        second = at_axis[axes[part][1]](second)
        if part == "A":
            return (second, third, first) + PART_A
        if part == "B":
            return (first, third, second) + PART_B
        return (second, first, third) + PART_C

    codes1 = {"A": ea1, "B": eb1, "C": ec1}
    codes2 = {"A": ea2, "B": eb2, "C": ec2}
    came1 = {"A": ra1, "B": rb1, "C": rc1}
    came2 = {"A": ra2, "B": rb2, "C": rc2}

    away = (2, -d, d, 0)
    behind = (0, d, -d, 2)

    copies = {}
    waited = set()

    def remote(name, src, dst, target):
        i = len(copies)
        copy = pltpu.make_async_remote_copy(
            src_ref=src, dst_ref=dst, send_sem=send.at[i], recv_sem=recv.at[i],
            device_id=target, device_id_type=MESH)
        copy.start()
        copies[name] = copy

    def arrived(*names):
        for name in names:
            if name not in waited:
                waited.add(name)
                copies[name].wait_recv()

    barrier = pltpu.get_barrier_semaphore()
    partners = [("x", k) for k in range(1, NX)] + [("y", k) for k in range(1, NY)]
    partners += [("z", k) for k in range(1, NZ)] + [("c", 1)]
    for axis, k in partners:
        pl.semaphore_signal(barrier, inc=1, device_id=to(axis, k), device_id_type=MESH)

    def strip(yy, core):
        return pl.ds(pl.multiple_of((yy // 2) * 4096 + core * 2048 + lax.rem(yy, 2) * 1024, 1024), 1024)

    def columns(yy):
        return pl.ds(pl.multiple_of(yy * 1024, 1024), 1024)

    own = [pltpu.make_async_copy(cot, cs.at[0], local.at[4])]
    for j in range(4):
        yy = py(away[j])
        own.append(pltpu.make_async_copy(inputs.at[:, :, strip(yy, c)], xs.at[0, :, :, columns(yy)], local.at[j]))
    for copy in own:
        copy.start()
    own_weight = pltpu.make_async_copy(weight, ws.at[y, z, x], local.at[5])
    own_weight.start()
    pl.semaphore_wait(barrier, len(partners))

    def start():
        for k in range(1, NX):
            remote(f"C1{k}", weight.at[PART_C], ws.at[(y, z, x) + PART_C], to("x", k))
        for k in range(1, NZ):
            remote(f"AB1{k}", weight.at[PART_AB], ws.at[(y, z, x) + PART_AB], to("z", k))
        remote("cot", cot, cs.at[1], to("c", 1))
        for j in range(4):
            yy = py((2, d, -d, 0)[j])
            remote(f"in{j}", inputs.at[:, :, strip(yy, 1 - c)], xs.at[1, :, :, columns(yy)], to("c", 1))

    def ring_start(part, j):
        axis = axes[part][0]
        ref = ws.at[at(part, 0, -behind[j])]
        remote(f"u{part}{j}0", ref, ref, to(axis, d))
        remote(f"d{part}{j}0", ref, ref, to(axis, -d))

    def head(part):
        if "weight" not in waited:
            waited.add("weight")
            own_weight.wait()
        if part == "C":
            arrived(*[f"C1{k}" for k in range(1, NX)])
        else:
            arrived(*[f"AB1{k}" for k in range(1, NZ)])
        ref = ws.at[at(part, 0, 0)]
        for j in (1, 2):
            remote(f"{part}2{j}", ref, ref, to(axes[part][1], behind[j]))
        ring_start(part, 0)

    def piece(part, j):
        arrived(f"{part}2{j}")
        if j == 1:
            ref = ws.at[at(part, 0, -d)]
            remote(f"{part}23", ref, ref, to(axes[part][1], d))
        ring_start(part, j)

    def hop(way, part, j, i):
        arrived(f"{way}{part}{j}{i - 1}")
        sign = d if way == "u" else -d
        ref = ws.at[at(part, -i * sign, -behind[j])]
        remote(f"{way}{part}{j}{i}", ref, ref, to(axes[part][0], sign))

    def gradient(j):
        if j == 0:
            own[0].wait()
            arrived("cot")
        own[1 + j].wait()
        arrived(f"in{j}")
        yy = py(away[j])

        @pl.loop(0, 2)
        def _(h):
            begin = pl.multiple_of(yy * 1024 + h * 512, 512)
            left = xs[:, :, :, pl.ds(begin, 512)].reshape(512, 512)
            right = cs[...].reshape(512, 512)
            out = lax.dot_general(left, right, (((0,), (0,)), ((), ())), preferred_element_type=F32)
            grad[yy, pl.ds(h * 4, 4)] = out.reshape(4, NX, ROWS, 512)

        if j < 2:
            for q in range(NX):
                total("B", (2, -d)[j], q, [], j)
        total("A", 2, j, [], 0)
        total("A", -d, j, [], 1)
        total("C", 4, j, [], 0)
        total("C", -3 * d, j, [], 4)

    ways = {"A": (d, -d, d), "B": (d, -d, d), "C": (d, d, d, d, -d, -d, -d)}

    def total(part, first, j, slots, send_slot):
        came = came1[part]

        def one(third):
            value = grad[at(part, first, away[j], third)]
            for slot in slots:
                value = value + decode(came[slot, j, third])
            if send_slot is None and j == 2:
                value = value + decode(came2[part][0, third])
            if send_slot is not None:
                codes1[part][send_slot, j, third] = encode(value)
            elif j < 3:
                codes2[part][j, third] = encode(value)
            else:
                grad[at(part, first, away[j], third)] = value

        if part == "C":
            one(ALL)
        else:
            @pl.loop(0, NZ // 4)
            def _(i):
                one(pl.ds(i * 4, 4))

        if send_slot is not None:
            remote(f"s{part}{j}{send_slot}", codes1[part].at[send_slot, j], came.at[send_slot, j],
                   to(axes[part][0], ways[part][send_slot]))
        elif j < 3:
            remote(f"v{part}{j}", codes2[part].at[j], came2[part].at[j], to(axes[part][1], (d, -d, d)[j]))

    def relay(part, j):
        arrived(f"s{part}{j}0")
        total(part, d, j, [0], 2)

    def relay_c(j, i):
        arrived(f"sC{j}{i - 1}")
        total("C", (4 - i) * d, j, [i - 1], i)
        if i < 3:
            arrived(f"sC{j}{3 + i}")
            total("C", -(3 - i) * d, j, [3 + i], 4 + i)

    def finish(part, j):
        slots = [3, 6] if part == "C" else [1, 2]
        arrived(*[f"s{part}{j}{slot}" for slot in slots])
        if j == 2:
            arrived(f"v{part}0")
        total(part, 0, j, slots, None)

    def second(part):
        arrived(f"v{part}1", f"v{part}2")
        came = came2[part]

        def one(third):
            where = at(part, 0, 0, third)
            grad[where] = grad[where] + (decode(came[1, third]) + decode(came[2, third]))

        if part == "C":
            one(ALL)
            for k in range(1, NX):
                ec3[k - 1] = encode(grad[(y, z, px(k)) + PART_C])
                remote(f"wC{k}", ec3.at[k - 1], rc3.at[k - 1], to("x", k))
        else:
            @pl.loop(0, NZ // 4)
            def _(i):
                one(pl.ds(i * 4, 4))

    def third():
        for k in range(1, NZ):
            eab3[k - 1] = encode(grad[(y, pz(k), x) + PART_AB])
            remote(f"w{k}", eab3.at[k - 1], rab3.at[k - 1], to("z", k))

    def last():
        arrived(*[f"wC{k}" for k in range(1, NX)])
        rows_c = grad[(y, z, x) + PART_C]
        for k in range(NX - 1):
            rows_c = rows_c + decode(rc3[k])
        weight_grad[:, 384:512] = rows_c * factor
        arrived(*[f"w{k}" for k in range(1, NZ)])
        rows_ab = grad[(y, z, x) + PART_AB]
        for k in range(NZ - 1):
            rows_ab = rows_ab + decode(rab3[k])
        weight_grad[:, 0:384] = rows_ab * factor

    def gathered(j):
        arrived(*[f"uA{j}{i}" for i in range(2)], f"dA{j}0")
        arrived(*[f"uC{j}{i}" for i in range(4)], *[f"dC{j}{i}" for i in range(3)])
        if j == 3:
            arrived(*[f"uB{q}1" for q in range(4)])
        elif j > 0:
            arrived(*[f"{' ud'[j]}B{q}0" for q in range(4)])

    def keys(j):
        gathered(j)
        yy = py(-behind[j])
        left = xs[:, :, :, columns(yy)].reshape(512, 1024)
        out = jnp.dot(left, ws[yy].reshape(1024, 512), preferred_element_type=F32).reshape(2, 2, 128, 512)
        if j == 0:
            acc[...] = out
        else:
            acc[...] += out
        if j == 3:
            remote("key", acc.at[1], key_in, to("c", 1))

    outs = []

    def back(j):
        gathered(j)
        yy = py(-behind[j])

        @pl.loop(0, 2)
        def _(h):
            right = ws[yy, pl.ds(h * 4, 4)].reshape(512, 512)
            out = lax.dot_general(cs[...].reshape(512, 512), right, (((1,), (1,)), ((), ())),
                                  preferred_element_type=F32).astype(BF16)
            stage[:, :, :, pl.ds(pl.multiple_of(j * 1024 + h * 512, 512), 512)] = out.reshape(2, 2, 128, 512)

        here = pl.ds(j * 1024, 1024)
        there = strip(yy, c)
        remote(f"out{j}", stage.at[1, :, :, here], input_grad.at[:, :, there], to("c", 1))
        copy = pltpu.make_async_copy(stage.at[0, :, :, here], input_grad.at[:, :, there], local.at[6 + j])
        copy.start()
        outs.append(copy)

    def close():
        arrived("key")
        key_out[...] = (acc[0] + key_in[...]).astype(BF16)
        for copy in outs:
            copy.wait()
        arrived(*[f"out{j}" for j in range(NY)])
        for copy in copies.values():
            copy.wait_send()

    steps = {"start": start, "t": third, "end": last, "z": close}
    for part in "ABC":
        steps[f"h{part}"] = functools.partial(head, part)
        steps[f"s{part}"] = functools.partial(second, part)
        for j in range(4):
            steps[f"g{part}{j}"] = functools.partial(piece, part, j)
            steps[f"r{part}{j}"] = functools.partial(relay, part, j)
            steps[f"f{part}{j}"] = functools.partial(finish, part, j)
            for i in range(1, 4):
                steps[f"u{part}{j}{i}"] = functools.partial(hop, "u", part, j, i)
                steps[f"d{part}{j}{i}"] = functools.partial(hop, "d", part, j, i)
    for j in range(4):
        steps[f"m{j}"] = functools.partial(gradient, j)
        steps[f"k{j}"] = functools.partial(keys, j)
        steps[f"i{j}"] = functools.partial(back, j)
        for i in range(1, 4):
            steps[f"c{j}{i}"] = functools.partial(relay_c, j, i)
    for name in ORDER:
        steps[name]()


def local(inputs, key_weight, key_cotangent):
    any_spec = pl.BlockSpec(memory_space=pl.ANY)
    vmem_spec = pl.BlockSpec(memory_space=pltpu.VMEM)
    codes = [
        pltpu.VMEM((3, NY, NZ, 16, 384), BF16),
        pltpu.VMEM((3, NX, NZ, 16, 384), BF16),
        pltpu.VMEM((7, NY, NX, 32, 128), BF16),
        pltpu.VMEM((3, NZ, 16, 384), BF16),
        pltpu.VMEM((3, NZ, 16, 384), BF16),
        pltpu.VMEM((3, NX, 32, 128), BF16),
        pltpu.VMEM((7, 32, 384), BF16),
        pltpu.VMEM((3, 32, 128), BF16),
    ]
    return pl.pallas_call(
        kernel,
        out_shape=(
            jax.ShapeDtypeStruct(key_cotangent.shape, BF16),
            jax.ShapeDtypeStruct(inputs.shape, BF16),
            jax.ShapeDtypeStruct(key_weight.shape, F32),
        ),
        in_specs=[any_spec, vmem_spec, any_spec],
        out_specs=(vmem_spec, any_spec, vmem_spec),
        scratch_shapes=[
            pltpu.VMEM((2, 2, 128, 4096), BF16),
            pltpu.VMEM((2, 2, 128, 512), BF16),
            pltpu.VMEM((NY, NZ, NX, ROWS, 512), BF16),
            pltpu.VMEM((NY, NZ, NX, ROWS, 512), F32),
            pltpu.VMEM((2, 2, 128, 512), F32),
            pltpu.VMEM((2, 128, 512), F32),
            pltpu.VMEM((2, 2, 128, 4096), BF16),
            *codes,
            *codes,
            pltpu.SemaphoreType.DMA((SEMS,)),
            pltpu.SemaphoreType.DMA((SEMS,)),
            pltpu.SemaphoreType.DMA((10,)),
        ],
        compiler_params=pltpu.CompilerParams(
            collective_id=0, has_side_effects=True, vmem_limit_bytes=47 * 2**20),
        cost_estimate=pl.CostEstimate(flops=3 * 2 * 256 * 8192 * 512, bytes_accessed=9 * 2**20, transcendentals=0),
        name="key_projection",
    )(inputs, key_weight, key_cotangent)


def solution(mesh):
    tokens = P(None, ("shard", "node"), None)
    rows = P(("node", "shard"), None)
    return jax.shard_map(local, mesh=mesh, in_specs=(tokens, rows, tokens),
                         out_specs=(tokens, tokens, rows), check_vma=False)
```

```python
import functools

import jax
import jax.numpy as jnp
from jax import lax
from jax.experimental import pallas as pl
from jax.experimental.pallas import tpu as pltpu
from jax.sharding import PartitionSpec as P

MESH = pl.DeviceIdType.MESH
F32 = jnp.float32
BF16 = jnp.bfloat16
ALL = slice(None)

NX, NY, NZ = 4, 4, 8
ROWS = 32


def place():
    s = lax.axis_index("shard")
    n = lax.axis_index("node")
    x = lax.rem(s, NX)
    z = lax.rem(s // NX, NZ)
    y = (n // 2) * 2 + s // (NX * NZ)
    return x, y, z, lax.rem(n, 2)


def device(x, y, z, c):
    return (lax.rem(y, 2) * (NX * NZ) + z * NX + x, (y // 2) * 2 + c)


PART_A = (pl.ds(0, 16), pl.ds(0, 384))
PART_B = (pl.ds(16, 16), pl.ds(0, 384))
PART_AB = (pl.ds(0, 32), pl.ds(0, 384))
PART_C = (pl.ds(0, 32), pl.ds(384, 128))

SEMS = 176

SCALE = 2.0 ** 8


def encode(value):
    square = value * value
    return ((value * jnp.abs(value)) * (square * SCALE ** 4)).astype(BF16)


def decode(code):
    power = code.astype(F32)
    root = lax.rsqrt(lax.rsqrt(jnp.abs(power))) * (1.0 / SCALE)
    return jnp.where(power < 0, -root, root)


ORDER = (
    "start", "hC", "m0", "hA", "uC01", "gC1", "m1", "m2", "hB", "dC01", "m3", "uC11", "uA01", "rA0",
    "rB0", "gC2", "c21", "c01", "rB3", "rB1", "rB2", "gC3", "c11", "uC02", "rA1", "c31", "gB1",
    "c22", "dC02", "gA1", "c02", "dC11", "uC21", "c12", "uC12", "uC31", "fB0", "rA3", "uC22", "rA2",
    "gA2", "dC12", "c23", "fA0", "c32", "gB3", "c03", "uA11", "fB1", "uC03", "uC32", "c13", "fA1",
    "gB2", "dC21", "uC13", "fB3", "dC31", "fA3", "c33", "fC0", "fA2", "fB2", "uB01", "gA3", "uB11",
    "dC22", "uA21", "k0", "i0", "uC33", "dC32", "uC23", "uB31", "fC3", "k1", "uB21", "fC1", "sB",
    "fC2", "uA31", "sA", "t", "i1", "k2", "i2", "k3", "sC", "i3", "end", "z",
)


def kernel(inputs, weight, cot, key_out, input_grad, weight_grad,
           xs, cs, ws, grad, acc, key_in, stage,
           ra1, rb1, rc1, ra2, rb2, rc2, rab3, rc3,
           ea1, eb1, ec1, ea2, eb2, ec2, eab3, ec3,
           send, recv, local):
    x, y, z, c = place()
    d = 1 - 2 * c
    factor = 1.0 / 256.0

    def px(k):
        return lax.rem(x + k + 4 * NX, NX)

    def py(k):
        return lax.rem(y + k + 4 * NY, NY)

    def pz(k):
        return lax.rem(z + k + 4 * NZ, NZ)

    def to(axis, k):
        if axis == "x":
            return device(px(k), y, z, c)
        if axis == "y":
            return device(x, py(k), z, c)
        if axis == "z":
            return device(x, y, pz(k), c)
        return device(x, y, z, 1 - c)

    axes = {"A": ("x", "y", "z"), "B": ("y", "x", "z"), "C": ("z", "y", "x")}
    at_axis = {"x": px, "y": py, "z": pz}

    def at(part, first, second, third=ALL):
        first = at_axis[axes[part][0]](first)
        second = at_axis[axes[part][1]](second)
        if part == "A":
            return (second, third, first) + PART_A
        if part == "B":
            return (first, third, second) + PART_B
        return (second, first, third) + PART_C

    codes1 = {"A": ea1, "B": eb1, "C": ec1}
    codes2 = {"A": ea2, "B": eb2, "C": ec2}
    came1 = {"A": ra1, "B": rb1, "C": rc1}
    came2 = {"A": ra2, "B": rb2, "C": rc2}

    away = (2, -d, d, 0)
    behind = (0, d, -d, 2)

    copies = {}
    waited = set()

    def remote(name, src, dst, target):
        i = len(copies)
        copy = pltpu.make_async_remote_copy(
            src_ref=src, dst_ref=dst, send_sem=send.at[i], recv_sem=recv.at[i],
            device_id=target, device_id_type=MESH)
        copy.start()
        copies[name] = copy

    def arrived(*names):
        for name in names:
            if name not in waited:
                waited.add(name)
                copies[name].wait_recv()

    barrier = pltpu.get_barrier_semaphore()
    partners = [("x", k) for k in range(1, NX)] + [("y", k) for k in range(1, NY)]
    partners += [("z", k) for k in range(1, NZ)] + [("c", 1)]
    for axis, k in partners:
        pl.semaphore_signal(barrier, inc=1, device_id=to(axis, k), device_id_type=MESH)

    def strip(yy, core):
        return pl.ds(pl.multiple_of((yy // 2) * 4096 + core * 2048 + lax.rem(yy, 2) * 1024, 1024), 1024)

    def columns(yy):
        return pl.ds(pl.multiple_of(yy * 1024, 1024), 1024)

    own = [pltpu.make_async_copy(cot, cs.at[0], local.at[4])]
    for j in range(4):
        yy = py(away[j])
        own.append(pltpu.make_async_copy(inputs.at[:, :, strip(yy, c)], xs.at[0, :, :, columns(yy)], local.at[j]))
    for copy in own:
        copy.start()
    own_weight = pltpu.make_async_copy(weight, ws.at[y, z, x], local.at[5])
    own_weight.start()
    pl.semaphore_wait(barrier, len(partners))

    def start():
        for k in range(1, NX):
            remote(f"C1{k}", weight.at[PART_C], ws.at[(y, z, x) + PART_C], to("x", k))
        for k in range(1, NZ):
            remote(f"AB1{k}", weight.at[PART_AB], ws.at[(y, z, x) + PART_AB], to("z", k))
        remote("cot", cot, cs.at[1], to("c", 1))
        for j in range(4):
            yy = py((2, d, -d, 0)[j])
            remote(f"in{j}", inputs.at[:, :, strip(yy, 1 - c)], xs.at[1, :, :, columns(yy)], to("c", 1))

    def ring_start(part, j):
        axis = axes[part][0]
        ref = ws.at[at(part, 0, -behind[j])]
        remote(f"u{part}{j}0", ref, ref, to(axis, d))
        remote(f"d{part}{j}0", ref, ref, to(axis, -d))

    def head(part):
        if "weight" not in waited:
            waited.add("weight")
            own_weight.wait()
        if part == "C":
            arrived(*[f"C1{k}" for k in range(1, NX)])
        else:
            arrived(*[f"AB1{k}" for k in range(1, NZ)])
        ref = ws.at[at(part, 0, 0)]
        for j in (1, 2):
            remote(f"{part}2{j}", ref, ref, to(axes[part][1], behind[j]))
        ring_start(part, 0)

    def piece(part, j):
        arrived(f"{part}2{j}")
        if j == 1:
            ref = ws.at[at(part, 0, -d)]
            remote(f"{part}23", ref, ref, to(axes[part][1], d))
        ring_start(part, j)

    def hop(way, part, j, i):
        arrived(f"{way}{part}{j}{i - 1}")
        sign = d if way == "u" else -d
        ref = ws.at[at(part, -i * sign, -behind[j])]
        remote(f"{way}{part}{j}{i}", ref, ref, to(axes[part][0], sign))

    def gradient(j):
        if j == 0:
            own[0].wait()
            arrived("cot")
        own[1 + j].wait()
        arrived(f"in{j}")
        yy = py(away[j])

        left = xs[:, :, :, columns(yy)].reshape(512, 1024)
        right = cs[...].reshape(512, 512)
        out = lax.dot_general(left, right, (((0,), (0,)), ((), ())), preferred_element_type=F32)
        grad[yy] = out.reshape(NZ, NX, ROWS, 512)

        if j < 2:
            for q in range(NX):
                total("B", (2, -d)[j], q, [], j)
        total("A", 2, j, [], 0)
        total("A", -d, j, [], 1)
        total("C", 4, j, [], 0)
        total("C", -3 * d, j, [], 4)

    ways = {"A": (d, -d, d), "B": (d, -d, d), "C": (d, d, d, d, -d, -d, -d)}

    def total(part, first, j, slots, send_slot):
        came = came1[part]

        def one(third):
            value = grad[at(part, first, away[j], third)]
            for slot in slots:
                value = value + decode(came[slot, j, third])
            if send_slot is None and j == 2:
                value = value + decode(came2[part][0, third])
            if send_slot is not None:
                codes1[part][send_slot, j, third] = encode(value)
            elif j < 3:
                codes2[part][j, third] = encode(value)
            else:
                grad[at(part, first, away[j], third)] = value

        if part == "C":
            one(ALL)
        else:
            @pl.loop(0, NZ // 4)
            def _(i):
                one(pl.ds(i * 4, 4))

        if send_slot is not None:
            remote(f"s{part}{j}{send_slot}", codes1[part].at[send_slot, j], came.at[send_slot, j],
                   to(axes[part][0], ways[part][send_slot]))
        elif j < 3:
            remote(f"v{part}{j}", codes2[part].at[j], came2[part].at[j], to(axes[part][1], (d, -d, d)[j]))

    def relay(part, j):
        arrived(f"s{part}{j}0")
        total(part, d, j, [0], 2)

    def relay_c(j, i):
        arrived(f"sC{j}{i - 1}")
        total("C", (4 - i) * d, j, [i - 1], i)
        if i < 3:
            arrived(f"sC{j}{3 + i}")
            total("C", -(3 - i) * d, j, [3 + i], 4 + i)

    def finish(part, j):
        slots = [3, 6] if part == "C" else [1, 2]
        arrived(*[f"s{part}{j}{slot}" for slot in slots])
        if j == 2:
            arrived(f"v{part}0")
        total(part, 0, j, slots, None)

    def second(part):
        arrived(f"v{part}1", f"v{part}2")
        came = came2[part]

        def one(third):
            where = at(part, 0, 0, third)
            grad[where] = grad[where] + (decode(came[1, third]) + decode(came[2, third]))

        if part == "C":
            one(ALL)
            for k in range(1, NX):
                ec3[k - 1] = encode(grad[(y, z, px(k)) + PART_C])
                remote(f"wC{k}", ec3.at[k - 1], rc3.at[k - 1], to("x", k))
        else:
            @pl.loop(0, NZ // 4)
            def _(i):
                one(pl.ds(i * 4, 4))

    def third():
        for k in range(1, NZ):
            eab3[k - 1] = encode(grad[(y, pz(k), x) + PART_AB])
            remote(f"w{k}", eab3.at[k - 1], rab3.at[k - 1], to("z", k))

    def last():
        arrived(*[f"wC{k}" for k in range(1, NX)])
        rows_c = grad[(y, z, x) + PART_C]
        for k in range(NX - 1):
            rows_c = rows_c + decode(rc3[k])
        weight_grad[:, 384:512] = rows_c * factor
        arrived(*[f"w{k}" for k in range(1, NZ)])
        rows_ab = grad[(y, z, x) + PART_AB]
        for k in range(NZ - 1):
            rows_ab = rows_ab + decode(rab3[k])
        weight_grad[:, 0:384] = rows_ab * factor

    def gathered(j):
        arrived(*[f"uA{j}{i}" for i in range(2)], f"dA{j}0")
        arrived(*[f"uC{j}{i}" for i in range(4)], *[f"dC{j}{i}" for i in range(3)])
        if j == 3:
            arrived(*[f"uB{q}1" for q in range(4)])
        elif j > 0:
            arrived(*[f"{' ud'[j]}B{q}0" for q in range(4)])

    def keys(j):
        gathered(j)
        yy = py(-behind[j])
        left = xs[:, :, :, columns(yy)].reshape(512, 1024)
        out = jnp.dot(left, ws[yy].reshape(1024, 512), preferred_element_type=F32).reshape(2, 2, 128, 512)
        if j == 0:
            acc[...] = out
        else:
            acc[...] += out
        if j == 3:
            remote("key", acc.at[1], key_in, to("c", 1))

    outs = []

    def back(j):
        gathered(j)
        yy = py(-behind[j])

        here = pl.ds(j * 1024, 1024)
        out = lax.dot_general(cs[...].reshape(512, 512), ws[yy].reshape(1024, 512), (((1,), (1,)), ((), ())),
                              preferred_element_type=F32).astype(BF16)
        stage[:, :, :, here] = out.reshape(2, 2, 128, 1024)
        there = strip(yy, c)
        remote(f"out{j}", stage.at[1, :, :, here], input_grad.at[:, :, there], to("c", 1))
        copy = pltpu.make_async_copy(stage.at[0, :, :, here], input_grad.at[:, :, there], local.at[6 + j])
        copy.start()
        outs.append(copy)

    def close():
        arrived("key")
        key_out[...] = (acc[0] + key_in[...]).astype(BF16)
        for copy in outs:
            copy.wait()
        arrived(*[f"out{j}" for j in range(NY)])
        for copy in copies.values():
            copy.wait_send()

    steps = {"start": start, "t": third, "end": last, "z": close}
    for part in "ABC":
        steps[f"h{part}"] = functools.partial(head, part)
        steps[f"s{part}"] = functools.partial(second, part)
        for j in range(4):
            steps[f"g{part}{j}"] = functools.partial(piece, part, j)
            steps[f"r{part}{j}"] = functools.partial(relay, part, j)
            steps[f"f{part}{j}"] = functools.partial(finish, part, j)
            for i in range(1, 4):
                steps[f"u{part}{j}{i}"] = functools.partial(hop, "u", part, j, i)
                steps[f"d{part}{j}{i}"] = functools.partial(hop, "d", part, j, i)
    for j in range(4):
        steps[f"m{j}"] = functools.partial(gradient, j)
        steps[f"k{j}"] = functools.partial(keys, j)
        steps[f"i{j}"] = functools.partial(back, j)
        for i in range(1, 4):
            steps[f"c{j}{i}"] = functools.partial(relay_c, j, i)
    for name in ORDER:
        steps[name]()


WRITES = 10


def write(key_in, grad_in, weight_in, key_out, input_grad, weight_grad, sems):
    copies = [pltpu.make_async_copy(key_in, key_out, sems.at[0]),
              pltpu.make_async_copy(weight_in, weight_grad, sems.at[1])]
    for i in range(8):
        part = (i // 4, pl.ds(i % 4 * 32, 32))
        copies.append(pltpu.make_async_copy(grad_in.at[part], input_grad.at[part], sems.at[2 + i]))
    for copy in copies:
        copy.start()
    for copy in copies:
        copy.wait()


def local(inputs, key_weight, key_cotangent):
    any_spec = pl.BlockSpec(memory_space=pl.ANY)
    vmem_spec = pl.BlockSpec(memory_space=pltpu.VMEM)
    codes = [
        pltpu.VMEM((3, NY, NZ, 16, 384), BF16),
        pltpu.VMEM((3, NX, NZ, 16, 384), BF16),
        pltpu.VMEM((7, NY, NX, 32, 128), BF16),
        pltpu.VMEM((3, NZ, 16, 384), BF16),
        pltpu.VMEM((3, NZ, 16, 384), BF16),
        pltpu.VMEM((3, NX, 32, 128), BF16),
        pltpu.VMEM((7, 32, 384), BF16),
        pltpu.VMEM((3, 32, 128), BF16),
    ]
    inputs, key_weight, key_cotangent = (
        pltpu.with_memory_space_constraint(v, pltpu.HBM) for v in (inputs, key_weight, key_cotangent))
    hbm_spec = pl.BlockSpec(memory_space=pltpu.HBM)
    results = pl.pallas_call(
        kernel,
        out_shape=(
            jax.ShapeDtypeStruct(key_cotangent.shape, BF16),
            jax.ShapeDtypeStruct(inputs.shape, BF16),
            jax.ShapeDtypeStruct(key_weight.shape, F32),
        ),
        in_specs=[hbm_spec, hbm_spec, hbm_spec],
        out_specs=(vmem_spec, any_spec, vmem_spec),
        scratch_shapes=[
            pltpu.VMEM((2, 2, 128, 4096), BF16),
            pltpu.VMEM((2, 2, 128, 512), BF16),
            pltpu.VMEM((NY, NZ, NX, ROWS, 512), BF16),
            pltpu.VMEM((NY, NZ, NX, ROWS, 512), F32),
            pltpu.VMEM((2, 2, 128, 512), F32),
            pltpu.VMEM((2, 128, 512), F32),
            pltpu.VMEM((2, 2, 128, 4096), BF16),
            *codes,
            *codes,
            pltpu.SemaphoreType.DMA((SEMS,)),
            pltpu.SemaphoreType.DMA((SEMS,)),
            pltpu.SemaphoreType.DMA((10,)),
        ],
        compiler_params=pltpu.CompilerParams(
            collective_id=0, has_side_effects=True, vmem_limit_bytes=47 * 2**20),
        cost_estimate=pl.CostEstimate(flops=3 * 2 * 256 * 8192 * 512, bytes_accessed=9 * 2**20, transcendentals=0),
        name="key_projection",
    )(inputs, key_weight, key_cotangent)
    return pl.pallas_call(
        write,
        out_shape=[jax.ShapeDtypeStruct(r.shape, r.dtype) for r in results],
        in_specs=[any_spec] * 3,
        out_specs=[any_spec] * 3,
        scratch_shapes=[pltpu.SemaphoreType.DMA((WRITES,))],
        cost_estimate=pl.CostEstimate(flops=0, bytes_accessed=9 * 2**20, transcendentals=0),
        compiler_params=pltpu.CompilerParams(vmem_limit_bytes=2**20),
        name="write_results",
    )(*results)


def solution(mesh):
    tokens = P(None, ("shard", "node"), None)
    rows = P(("node", "shard"), None)
    return jax.shard_map(local, mesh=mesh, in_specs=(tokens, rows, tokens),
                         out_specs=(tokens, tokens, rows), check_vma=False)
```

```python
import functools

import jax
import jax.numpy as jnp
from jax import lax
from jax.experimental import pallas as pl
from jax.experimental.pallas import tpu as pltpu
from jax.sharding import PartitionSpec as P

MESH = pl.DeviceIdType.MESH
F32 = jnp.float32
BF16 = jnp.bfloat16
ALL = slice(None)

NX, NY, NZ = 4, 4, 8
ROWS = 32


def place():
    s = lax.axis_index("shard")
    n = lax.axis_index("node")
    x = lax.rem(s, NX)
    z = lax.rem(s // NX, NZ)
    y = (n // 2) * 2 + s // (NX * NZ)
    return x, y, z, lax.rem(n, 2)


def device(x, y, z, c):
    return (lax.rem(y, 2) * (NX * NZ) + z * NX + x, (y // 2) * 2 + c)


PART_A = (pl.ds(0, 16), pl.ds(0, 384))
PART_B = (pl.ds(16, 16), pl.ds(0, 384))
PART_AB = (pl.ds(0, 32), pl.ds(0, 384))
PART_C = (pl.ds(0, 32), pl.ds(384, 128))

SEMS = 192

SCALE = 2.0 ** 8


def encode(value):
    square = value * value
    return ((value * jnp.abs(value)) * (square * SCALE ** 4)).astype(BF16)


def decode(code):
    power = code.astype(F32)
    root = lax.rsqrt(lax.rsqrt(jnp.abs(power))) * (1.0 / SCALE)
    return jnp.where(power < 0, -root, root)


ORDER = (
    "start", "hC", "m0", "hA", "uC01", "gC1", "m1", "m2", "hB", "dC01", "m3", "uC11", "uA01", "rA0",
    "rB0", "gC2", "c21", "c01", "rB3", "rB1", "rB2", "gC3", "c11", "uC02", "rA1", "c31", "gB1",
    "c22", "dC02", "gA1", "c02", "dC11", "uC21", "c12", "uC12", "uC31", "fB0", "rA3", "uC22", "rA2",
    "gA2", "dC12", "c23", "fA0", "c32", "gB3", "c03", "uA11", "fB1", "uC03", "uC32", "c13", "fA1",
    "gB2", "dC21", "uC13", "fB3", "dC31", "fA3", "c33", "fC0", "fA2", "fB2", "uB01", "gA3", "uB11",
    "dC22", "uA21", "k0", "i0", "uC33", "dC32", "uC23", "uB31", "fC3", "k1", "uB21", "fC1", "sB",
    "tB", "fC2", "uA31", "sA", "tA", "i1", "k2", "i2", "k3", "sC", "i3", "end", "z",
)


def kernel(inputs, weight, cot, key_out, input_grad, weight_grad,
           xs, cs, ws, grad, acc, key_in, stage,
           ra1, rb1, rc1, ra2, rb2, rc2, rab3, rc3,
           ea1, eb1, ec1, ea2, eb2, ec2, eab3, ec3,
           send, recv, local):
    x, y, z, c = place()
    d = 1 - 2 * c
    factor = 1.0 / 256.0

    def px(k):
        return lax.rem(x + k + 4 * NX, NX)

    def py(k):
        return lax.rem(y + k + 4 * NY, NY)

    def pz(k):
        return lax.rem(z + k + 4 * NZ, NZ)

    def to(axis, k):
        if axis == "x":
            return device(px(k), y, z, c)
        if axis == "y":
            return device(x, py(k), z, c)
        if axis == "z":
            return device(x, y, pz(k), c)
        return device(x, y, z, 1 - c)

    axes = {"A": ("x", "y", "z"), "B": ("y", "x", "z"), "C": ("z", "y", "x")}
    at_axis = {"x": px, "y": py, "z": pz}

    def at(part, first, second, third=ALL):
        first = at_axis[axes[part][0]](first)
        second = at_axis[axes[part][1]](second)
        if part == "A":
            return (second, third, first) + PART_A
        if part == "B":
            return (first, third, second) + PART_B
        return (second, first, third) + PART_C

    codes1 = {"A": ea1, "B": eb1, "C": ec1}
    codes2 = {"A": ea2, "B": eb2, "C": ec2}
    came1 = {"A": ra1, "B": rb1, "C": rc1}
    came2 = {"A": ra2, "B": rb2, "C": rc2}

    away = (2, -d, d, 0)
    behind = (0, d, -d, 2)

    copies = {}
    waited = set()

    def remote(name, src, dst, target):
        i = len(copies)
        copy = pltpu.make_async_remote_copy(
            src_ref=src, dst_ref=dst, send_sem=send.at[i], recv_sem=recv.at[i],
            device_id=target, device_id_type=MESH)
        copy.start()
        copies[name] = copy

    def arrived(*names):
        for name in names:
            if name not in waited:
                waited.add(name)
                copies[name].wait_recv()

    barrier = pltpu.get_barrier_semaphore()
    partners = [("x", k) for k in range(1, NX)] + [("y", k) for k in range(1, NY)]
    partners += [("z", k) for k in range(1, NZ)] + [("c", 1)]
    for axis, k in partners:
        pl.semaphore_signal(barrier, inc=1, device_id=to(axis, k), device_id_type=MESH)

    def strip(yy, core):
        return pl.ds(pl.multiple_of((yy // 2) * 4096 + core * 2048 + lax.rem(yy, 2) * 1024, 1024), 1024)

    def columns(yy):
        return pl.ds(pl.multiple_of(yy * 1024, 1024), 1024)

    own = [pltpu.make_async_copy(cot, cs.at[0], local.at[4])]
    for j in range(4):
        yy = py(away[j])
        own.append(pltpu.make_async_copy(inputs.at[:, :, strip(yy, c)], xs.at[0, :, :, columns(yy)], local.at[j]))
    for copy in own:
        copy.start()
    own_weight = pltpu.make_async_copy(weight, ws.at[y, z, x], local.at[5])
    own_weight.start()
    own_weight.wait()
    pl.semaphore_wait(barrier, len(partners))

    def start():
        for k in range(1, NX):
            remote(f"C1{k}", ws.at[(y, z, x) + PART_C], ws.at[(y, z, x) + PART_C], to("x", k))
        for k in range(1, NZ):
            remote(f"AB1{k}", ws.at[(y, z, x) + PART_AB], ws.at[(y, z, x) + PART_AB], to("z", k))
        remote("cot", cot, cs.at[1], to("c", 1))
        for j in range(4):
            yy = py((2, d, -d, 0)[j])
            remote(f"in{j}", inputs.at[:, :, strip(yy, 1 - c)], xs.at[1, :, :, columns(yy)], to("c", 1))

    def ring_start(part, j):
        axis = axes[part][0]
        ref = ws.at[at(part, 0, -behind[j])]
        remote(f"u{part}{j}0", ref, ref, to(axis, d))
        remote(f"d{part}{j}0", ref, ref, to(axis, -d))

    def head(part):
        if part == "C":
            arrived(*[f"C1{k}" for k in range(1, NX)])
        else:
            arrived(*[f"AB1{k}" for k in range(1, NZ)])
        ref = ws.at[at(part, 0, 0)]
        for j in (1, 2):
            remote(f"{part}2{j}", ref, ref, to(axes[part][1], behind[j]))
        ring_start(part, 0)

    def piece(part, j):
        arrived(f"{part}2{j}")
        if j == 1:
            ref = ws.at[at(part, 0, -d)]
            remote(f"{part}23", ref, ref, to(axes[part][1], d))
        ring_start(part, j)

    def hop(way, part, j, i):
        arrived(f"{way}{part}{j}{i - 1}")
        sign = d if way == "u" else -d
        ref = ws.at[at(part, -i * sign, -behind[j])]
        remote(f"{way}{part}{j}{i}", ref, ref, to(axes[part][0], sign))

    def gradient(j):
        if j == 0:
            own[0].wait()
            arrived("cot")
        own[1 + j].wait()
        arrived(f"in{j}")
        yy = py(away[j])

        left = xs[:, :, :, columns(yy)].reshape(512, 1024)
        right = cs[...].reshape(512, 512)
        out = lax.dot_general(left, right, (((0,), (0,)), ((), ())), preferred_element_type=F32)
        grad[yy] = out.reshape(NZ, NX, ROWS, 512)

        if j < 2:
            for q in range(NX):
                total("B", (2, -d)[j], q, [], j)
        total("A", 2, j, [], 0)
        total("A", -d, j, [], 1)
        total("C", 4, j, [], 0)
        total("C", -3 * d, j, [], 4)

    ways = {"A": (d, -d, d), "B": (d, -d, d), "C": (d, d, d, d, -d, -d, -d)}

    def total(part, first, j, slots, send_slot):
        came = came1[part]

        def one(third):
            value = grad[at(part, first, away[j], third)]
            for slot in slots:
                value = value + decode(came[slot, j, third])
            if send_slot is None and j == 2:
                value = value + decode(came2[part][0, third])
            if send_slot is not None:
                codes1[part][send_slot, j, third] = encode(value)
            elif j < 3:
                codes2[part][j, third] = encode(value)
            else:
                grad[at(part, first, away[j], third)] = value

        if part == "C":
            one(ALL)
        else:
            @pl.loop(0, NZ // 4)
            def _(i):
                one(pl.ds(i * 4, 4))

        if send_slot is not None:
            remote(f"s{part}{j}{send_slot}", codes1[part].at[send_slot, j], came.at[send_slot, j],
                   to(axes[part][0], ways[part][send_slot]))
        elif j < 3:
            remote(f"v{part}{j}", codes2[part].at[j], came2[part].at[j], to(axes[part][1], (d, -d, d)[j]))

    def relay(part, j):
        arrived(f"s{part}{j}0")
        total(part, d, j, [0], 2)

    def relay_c(j, i):
        arrived(f"sC{j}{i - 1}")
        total("C", (4 - i) * d, j, [i - 1], i)
        if i < 3:
            arrived(f"sC{j}{3 + i}")
            total("C", -(3 - i) * d, j, [3 + i], 4 + i)

    def finish(part, j):
        slots = [3, 6] if part == "C" else [1, 2]
        arrived(*[f"s{part}{j}{slot}" for slot in slots])
        if j == 2:
            arrived(f"v{part}0")
        total(part, 0, j, slots, None)

    def second(part):
        arrived(f"v{part}1", f"v{part}2")
        came = came2[part]

        def one(third):
            where = at(part, 0, 0, third)
            grad[where] = grad[where] + (decode(came[1, third]) + decode(came[2, third]))

        if part == "C":
            one(ALL)
            for k in range(1, NX):
                ec3[k - 1] = encode(grad[(y, z, px(k)) + PART_C])
                remote(f"wC{k}", ec3.at[k - 1], rc3.at[k - 1], to("x", k))
        else:
            @pl.loop(0, NZ // 4)
            def _(i):
                one(pl.ds(i * 4, 4))

    def third(part):
        rows, cols = PART_A if part == "A" else PART_B
        for k in range(1, NZ):
            eab3[k - 1, rows] = encode(grad[y, pz(k), x, rows, cols])
            remote(f"w{part}{k}", eab3.at[k - 1, rows], rab3.at[k - 1, rows], to("z", k))

    def last():
        arrived(*[f"wC{k}" for k in range(1, NX)])
        rows_c = grad[(y, z, x) + PART_C]
        for k in range(NX - 1):
            rows_c = rows_c + decode(rc3[k])
        weight_grad[:, 384:512] = rows_c * factor
        arrived(*[f"w{part}{k}" for part in "AB" for k in range(1, NZ)])
        rows_ab = grad[(y, z, x) + PART_AB]
        for k in range(NZ - 1):
            rows_ab = rows_ab + decode(rab3[k])
        weight_grad[:, 0:384] = rows_ab * factor

    def gathered(j):
        arrived(*[f"uA{j}{i}" for i in range(2)], f"dA{j}0")
        arrived(*[f"uC{j}{i}" for i in range(4)], *[f"dC{j}{i}" for i in range(3)])
        if j == 3:
            arrived(*[f"uB{q}1" for q in range(4)])
        elif j > 0:
            arrived(*[f"{' ud'[j]}B{q}0" for q in range(4)])

    def keys(j):
        gathered(j)
        yy = py(-behind[j])
        right = ws[yy].reshape(1024, 512)
        for who in (1, 0):
            left = xs[who, :, :, columns(yy)].reshape(256, 1024)
            out = jnp.dot(left, right, preferred_element_type=F32).reshape(2, 128, 512)
            if j == 0:
                acc[who] = out
            else:
                acc[who] += out
            if j == 3 and who == 1:
                remote("key", acc.at[1], key_in, to("c", 1))

    outs = []

    def back(j):
        gathered(j)
        yy = py(-behind[j])

        here = pl.ds(j * 1024, 1024)
        there = strip(yy, c)
        right = ws[yy].reshape(1024, 512)
        for who in (1, 0):
            out = lax.dot_general(cs[who].reshape(256, 512), right, (((1,), (1,)), ((), ())),
                                  preferred_element_type=F32).astype(BF16)
            stage[who, :, :, here] = out.reshape(2, 128, 1024)
            if who == 1:
                remote(f"out{j}", stage.at[1, :, :, here], input_grad.at[:, :, there], to("c", 1))
        copy = pltpu.make_async_copy(stage.at[0, :, :, here], input_grad.at[:, :, there], local.at[6 + j])
        copy.start()
        outs.append(copy)

    def close():
        arrived("key")
        key_out[...] = (acc[0] + key_in[...]).astype(BF16)
        for copy in outs:
            copy.wait()
        arrived(*[f"out{j}" for j in range(NY)])
        for copy in copies.values():
            copy.wait_send()

    steps = {"start": start, "end": last, "z": close}
    for part in "ABC":
        steps[f"h{part}"] = functools.partial(head, part)
        steps[f"s{part}"] = functools.partial(second, part)
        steps[f"t{part}"] = functools.partial(third, part)
        for j in range(4):
            steps[f"g{part}{j}"] = functools.partial(piece, part, j)
            steps[f"r{part}{j}"] = functools.partial(relay, part, j)
            steps[f"f{part}{j}"] = functools.partial(finish, part, j)
            for i in range(1, 4):
                steps[f"u{part}{j}{i}"] = functools.partial(hop, "u", part, j, i)
                steps[f"d{part}{j}{i}"] = functools.partial(hop, "d", part, j, i)
    for j in range(4):
        steps[f"m{j}"] = functools.partial(gradient, j)
        steps[f"k{j}"] = functools.partial(keys, j)
        steps[f"i{j}"] = functools.partial(back, j)
        for i in range(1, 4):
            steps[f"c{j}{i}"] = functools.partial(relay_c, j, i)
    for name in ORDER:
        steps[name]()


WRITES = 10


def write(key_in, grad_in, weight_in, key_out, input_grad, weight_grad, sems):
    copies = [pltpu.make_async_copy(key_in, key_out, sems.at[0]),
              pltpu.make_async_copy(weight_in, weight_grad, sems.at[1])]
    for i in range(8):
        part = (i // 4, pl.ds(i % 4 * 32, 32))
        copies.append(pltpu.make_async_copy(grad_in.at[part], input_grad.at[part], sems.at[2 + i]))
    for copy in copies:
        copy.start()
    for copy in copies:
        copy.wait()


def local(inputs, key_weight, key_cotangent):
    any_spec = pl.BlockSpec(memory_space=pl.ANY)
    vmem_spec = pl.BlockSpec(memory_space=pltpu.VMEM)
    codes = [
        pltpu.VMEM((3, NY, NZ, 16, 384), BF16),
        pltpu.VMEM((3, NX, NZ, 16, 384), BF16),
        pltpu.VMEM((7, NY, NX, 32, 128), BF16),
        pltpu.VMEM((3, NZ, 16, 384), BF16),
        pltpu.VMEM((3, NZ, 16, 384), BF16),
        pltpu.VMEM((3, NX, 32, 128), BF16),
        pltpu.VMEM((7, 32, 384), BF16),
        pltpu.VMEM((3, 32, 128), BF16),
    ]
    inputs, key_weight, key_cotangent = (
        pltpu.with_memory_space_constraint(v, pltpu.HBM) for v in (inputs, key_weight, key_cotangent))
    hbm_spec = pl.BlockSpec(memory_space=pltpu.HBM)
    results = pl.pallas_call(
        kernel,
        out_shape=(
            jax.ShapeDtypeStruct(key_cotangent.shape, BF16),
            jax.ShapeDtypeStruct(inputs.shape, BF16),
            jax.ShapeDtypeStruct(key_weight.shape, F32),
        ),
        in_specs=[hbm_spec, hbm_spec, hbm_spec],
        out_specs=(vmem_spec, any_spec, vmem_spec),
        scratch_shapes=[
            pltpu.VMEM((2, 2, 128, 4096), BF16),
            pltpu.VMEM((2, 2, 128, 512), BF16),
            pltpu.VMEM((NY, NZ, NX, ROWS, 512), BF16),
            pltpu.VMEM((NY, NZ, NX, ROWS, 512), F32),
            pltpu.VMEM((2, 2, 128, 512), F32),
            pltpu.VMEM((2, 128, 512), F32),
            pltpu.VMEM((2, 2, 128, 4096), BF16),
            *codes,
            *codes,
            pltpu.SemaphoreType.DMA((SEMS,)),
            pltpu.SemaphoreType.DMA((SEMS,)),
            pltpu.SemaphoreType.DMA((10,)),
        ],
        compiler_params=pltpu.CompilerParams(
            collective_id=0, has_side_effects=True, vmem_limit_bytes=47 * 2**20),
        cost_estimate=pl.CostEstimate(flops=3 * 2 * 256 * 8192 * 512, bytes_accessed=9 * 2**20, transcendentals=0),
        name="key_projection",
    )(inputs, key_weight, key_cotangent)
    return pl.pallas_call(
        write,
        out_shape=[jax.ShapeDtypeStruct(r.shape, r.dtype) for r in results],
        in_specs=[any_spec] * 3,
        out_specs=[any_spec] * 3,
        scratch_shapes=[pltpu.SemaphoreType.DMA((WRITES,))],
        cost_estimate=pl.CostEstimate(flops=0, bytes_accessed=9 * 2**20, transcendentals=0),
        compiler_params=pltpu.CompilerParams(vmem_limit_bytes=2**20),
        name="write_results",
    )(*results)


def solution(mesh):
    tokens = P(None, ("shard", "node"), None)
    rows = P(("node", "shard"), None)
    return jax.shard_map(local, mesh=mesh, in_specs=(tokens, rows, tokens),
                         out_specs=(tokens, tokens, rows), check_vma=False)
```
